32 devices in a mesh: groups: 2 (over x), din: 8 (over z, y), dout: 2 (over core).
Axes of the slice: x: 2, y: 2, z: 4, core: 2. Of those that a mesh axis runs over, the one named last changes fastest.
Arguments:
- tokens: bfloat16 [2048, 16384], P(('groups', 'din'), 'dout'), parts along dimension 0, may hold values from -6 to 6
- w_query: bfloat16 [16384, 8192], P('dout', 'din'), may hold values from -0.046875 to 0.046875
- w_key: bfloat16 [16384, 512], P('dout', 'din'), may hold values from -0.046875 to 0.046875
- w_value: bfloat16 [16384, 512], P('dout', 'din'), may hold values from -0.046875 to 0.046875
- w_out: bfloat16 [8192, 16384], P('din', 'dout'), may hold values from -1 to 1
- k_cache: bfloat16 [8, 2048, 128], P('groups', 'din'), parts along dimension 0, may hold values from -1000 to 1000
- v_cache: bfloat16 [8, 2048, 128], P('groups', 'din'), parts along dimension 0, may hold values from -6 to 6
- span_start: int32 [2], P('groups'), parts along dimension 0, may hold values from 1 to 2048
Outputs:
- attended: bfloat16 [2048, 16384], P(('groups', 'din'), 'dout'), parts along dimension 0
The draws below stay inside these ranges and needn't reach their ends.
There are 2 independent parts, one for each index of `groups`. The reference program is written for one: setup_inputs(seed, part) draws one part's arguments, and reference() takes and returns one part's arrays. A program takes and returns all parts, laid end to end along the dimension named above; an argument that names none is the same for every part. Nothing has to cross between parts.
All inputs are finite; a program needn't handle non-finite values.
Results may differ from the reference program's by a relative error of at most 0.014.
The reference program's roundings to bfloat16 on the way (of `queries`, `new_keys`, `new_values`, `weights` and `heads_out`) count: a program that leaves them out, or rounds other values in their place, can miss the bound.
Values may be sent and summed in bfloat16 or wider, within the bound.
A program may use at most 192 MiB of HBM per device.

```python
import math
import jax
import jax.numpy as jnp
from jax import lax

D = 16384
HEADS = 64
KVH = 4
HD = 128
SPAN = 1024
CACHE = 2048


def draw_k_cache(key, part):
    key = jax.random.fold_in(key, 11)
    base = jnp.clip(jax.random.normal(key, (KVH, CACHE, HD), jnp.float32), -6.0, 6.0) * 1.5
    return base.astype(jnp.bfloat16)


def levels(own_key, extent, pieces, low, top_value):
    def one(dim, shards_of):
        steps = jax.random.uniform(jax.random.fold_in(jax.random.fold_in(own_key, 6), dim), (shards_of,), jnp.float32, low / len(pieces), top_value / len(pieces))
        return jnp.repeat(jnp.exp(steps), extent[dim] // shards_of).reshape((-1,) + (1,) * (len(extent) - dim - 1))

    loudness = one(*pieces[0])
    for cut in pieces[1:]:
        loudness = loudness * one(*cut)
    return loudness


def scatter_about(stream_key, shape, spread, most, pieces=(), kind=jnp.bfloat16):
    drawn = jax.random.normal(stream_key, shape, jnp.float32) * spread
    if len(pieces) > 0:
        drawn = levels(stream_key, shape, pieces, -0.22, 0.18) * drawn
    return jnp.clip(drawn, min=-most, max=most).astype(kind)


def setup_inputs(seed: int = 0, part: int = 0) -> dict:
    seeds = jax.random.split(jax.random.key(seed), 9)
    part_keys = jax.random.split(jax.random.fold_in(seeds[8], part), 9)
    tokens = scatter_about(part_keys[0], (SPAN, D), 1.0, 6.0, ((0, 8), (1, 2)))
    w_query = scatter_about(seeds[1], (D, HEADS * HD), D ** -0.5, 0.046875, ((0, 2), (1, 8)))
    w_key = scatter_about(seeds[2], (D, KVH * HD), D ** -0.5, 0.046875, ((0, 2), (1, 8)))
    w_value = scatter_about(seeds[3], (D, KVH * HD), D ** -0.5, 0.046875, ((0, 2), (1, 8)))
    w_out = scatter_about(seeds[4], (HEADS * HD, D), (max(HEADS * HD // 256, 1)) ** -0.5, 1.0, ((0, 8), (1, 2)))
    k_cache = draw_k_cache(jax.random.fold_in(jax.random.fold_in(seeds[8], part), 71), part)
    v_cache = scatter_about(part_keys[6], (KVH, CACHE, HD), 1.0, 6.0, ((1, 8),))
    span_start = jax.random.randint(part_keys[7], (1,), 1, CACHE + 1).astype(jnp.int32)
    return {"tokens": tokens, "w_query": w_query, "w_key": w_key, "w_value": w_value, "w_out": w_out, "k_cache": k_cache, "v_cache": v_cache, "span_start": span_start}


rope_base = 500000.0


def rotate(values, positions):
    half = values.shape[-1] // 2
    freq = jnp.exp(jnp.arange(half, dtype=jnp.float32) * (-2.0 * math.log(rope_base) / values.shape[-1]))
    angle = positions.astype(jnp.float32)[:, None] * freq[None, :]
    cosine = jnp.cos(angle)
    sine = jnp.sin(angle)
    first = values[..., :half]
    second = values[..., half:]
    return jnp.concatenate([first * cosine - second * sine, second * cosine + first * sine], -1)


def reference(tokens, w_query, w_key, w_value, w_out, k_cache, v_cache, span_start):
    scale = HD ** -0.5
    start_pos = span_start[0]
    positions = start_pos + jnp.arange(SPAN, dtype=jnp.int32)
    queries = jnp.dot(tokens, w_query, preferred_element_type=jnp.float32).reshape(SPAN, HEADS, HD).transpose(1, 0, 2)
    queries = rotate(queries, positions).astype(jnp.bfloat16)
    new_keys = jnp.dot(tokens, w_key, preferred_element_type=jnp.float32).reshape(SPAN, KVH, HD).transpose(1, 0, 2)
    new_keys = rotate(new_keys, positions).astype(jnp.bfloat16)
    new_values = jnp.dot(tokens, w_value, preferred_element_type=jnp.float32).reshape(SPAN, KVH, HD).transpose(1, 0, 2)
    new_values = new_values.astype(jnp.bfloat16)
    all_keys = jnp.concatenate([k_cache, new_keys], 1)
    all_values = jnp.concatenate([v_cache, new_values], 1)
    slots = jnp.arange(CACHE + SPAN, dtype=jnp.int32)
    rows = jnp.arange(SPAN, dtype=jnp.int32)
    allowed = jnp.where(slots[None, :] < CACHE, slots[None, :] < start_pos, slots[None, :] - CACHE <= rows[:, None])

    def one_head(item):
        query, head = item
        group_id = head % KVH
        head_keys = lax.dynamic_index_in_dim(all_keys, group_id, 0, keepdims=False)
        head_values = lax.dynamic_index_in_dim(all_values, group_id, 0, keepdims=False)
        scores = jnp.dot(query, head_keys.T, preferred_element_type=jnp.float32) * scale
        scores = jnp.where(allowed, scores, -jnp.inf)
        peak = jnp.max(scores, -1)
        weights = jnp.exp(scores - peak[:, None])
        total = jnp.sum(weights, -1)
        weighted = jnp.dot(weights.astype(jnp.bfloat16), head_values, preferred_element_type=jnp.float32)
        return (weighted / total[:, None]).astype(jnp.bfloat16)

    heads_out = lax.map(one_head, (queries, jnp.arange(HEADS, dtype=jnp.int32)))
    merged = heads_out.transpose(1, 0, 2).reshape(SPAN, HEADS * HD)
    return jnp.dot(merged, w_out, preferred_element_type=jnp.float32).astype(jnp.bfloat16)
```

```python
import functools
import math

import jax
import jax.numpy as jnp
from jax import lax
from jax.experimental import pallas as pl
from jax.experimental.pallas import tpu as pltpu
from jax.sharding import PartitionSpec as P

rope_base = 500000.0
MESH = pl.DeviceIdType.MESH
VMEM_BYTES = 60 * 2**20


def ring_index(pos, n, snake):
    if not snake:
        return pos
    high = pos // (n // 2)
    return (1 - high) * 2 * pos + high * (2 * (n - 1 - pos) + 1)


def ring_place(index, n, snake):
    if not snake:
        return index
    odd = index % 2
    return (1 - odd) * (index // 2) + odd * (n - 1 - index // 2)


def enter(right, left, core):
    barrier = pltpu.get_barrier_semaphore()
    for target in ({"din": right}, {"din": left}, {"dout": 1 - core}):
        pl.semaphore_signal(barrier, inc=1, device_id=target, device_id_type=MESH)
    pl.semaphore_wait(barrier, 3)


def rope_tables(positions, head_size):
    half = head_size // 2
    freq = jnp.exp(
        jnp.arange(half, dtype=jnp.float32) * (-2.0 * math.log(rope_base) / head_size)
    )
    angle = positions.astype(jnp.float32)[:, None] * freq[None, :]
    return jnp.cos(angle), jnp.sin(angle)


def rotate(values, cosine, sine):
    half = values.shape[-1] // 2
    first = values[..., :half]
    second = values[..., half:]
    return jnp.concatenate([first * cosine - second * sine, second * cosine + first * sine], -1)


def gather_kernel(
    n, snake, pair,
    x_ref, wq_hbm, wkv_hbm, k_ref, v_ref,
    out_ref, kc_ref, vc_ref,
    buf, wq, wkv, part, other,
    local_sem, send_sem, recv_sem, pair_send, pair_recv,
):
    core = lax.axis_index("dout")
    me_index = lax.axis_index("din")
    me = ring_place(me_index, n, snake)
    at = lambda pos: ring_index(lax.rem(pos + 2 * n, n), n, snake)
    right, left = at(me + 1), at(me - 1)
    rows = x_ref.shape[0]
    half = rows // 2
    slots = k_ref.shape[1]
    heads = kc_ref.shape[0]
    cols = wq.shape[1]
    own_cols = cols // 2
    steps = n // 2

    mine_heads = pl.ds(core * heads, heads)
    first = [
        x_ref.at[pl.ds(0, half)],
        k_ref.at[mine_heads],
        x_ref.at[pl.ds(half, half)],
        v_ref.at[mine_heads],
    ]

    def place(index, piece):
        if piece == 0:
            return buf.at[index, pl.ds(0, half)]
        if piece == 2:
            return buf.at[index, pl.ds(half, half)]
        ref = kc_ref if piece == 1 else vc_ref
        return ref.at[:, pl.ds(pl.multiple_of(index * slots, slots), slots)]

    locals_ = [
        pltpu.make_async_copy(first[piece], place(me_index, piece), local_sem.at[piece])
        for piece in range(4)
    ] + [
        pltpu.make_async_copy(wq_hbm, wq, local_sem.at[4]),
        pltpu.make_async_copy(wkv_hbm, wkv, local_sem.at[5]),
    ]

    def copy(way, step, piece):
        index = at(me - step if way == 0 else me + step)
        return pltpu.make_async_remote_copy(
            src_ref=first[piece] if step == 0 else place(index, piece),
            dst_ref=place(index, piece),
            send_sem=send_sem.at[way, step, piece],
            recv_sem=recv_sem.at[way, step, piece],
            device_id={"din": right if way == 0 else left},
            device_id_type=MESH,
        )

    def arrival(way, step, piece):
        index = at(me - 1 - step if way == 0 else me + 1 + step)
        return pltpu.make_async_remote_copy(
            src_ref=place(index, piece),
            dst_ref=place(index, piece),
            send_sem=send_sem.at[way, step, piece],
            recv_sem=recv_sem.at[way, step, piece],
            device_id={"din": right if way == 0 else left},
            device_id_type=MESH,
        )

    def travels(way, step, piece):
        return step < steps - 1 or (piece // 2 == way)

    def swap(order, index):
        at_rows = pl.ds(pl.multiple_of(index * rows, rows), rows)
        return pltpu.make_async_remote_copy(
            src_ref=part.at[at_rows],
            dst_ref=other.at[at_rows],
            send_sem=pair_send.at[order],
            recv_sem=pair_recv.at[order],
            device_id={"dout": 1 - core},
            device_id_type=MESH,
        )

    def project(order, index):
        at_rows = pl.ds(pl.multiple_of(index * rows, rows), rows)

        @pl.loop(0, own_cols // pair)
        def _(m):
            to = pl.ds(pl.multiple_of(m * pair, pair), pair)
            mine = pl.ds(pl.multiple_of((2 * m + core) * pair, pair), pair)
            theirs = pl.ds(pl.multiple_of((2 * m + 1 - core) * pair, pair), pair)
            part[at_rows, to] = jnp.dot(
                buf[index], wq[:, theirs], preferred_element_type=jnp.float32
            )
            out_ref[at_rows, to] = jnp.dot(
                buf[index], wq[:, mine], preferred_element_type=jnp.float32
            )

        both = jnp.dot(buf[index], wkv[...], preferred_element_type=jnp.float32)
        part[at_rows, own_cols:] = both
        out_ref[at_rows, own_cols:] = both
        swap(order, index).start()

    for item in locals_:
        item.start()
    enter(right, left, core)

    order = 0
    swaps = []
    for step in range(steps):
        for piece in range(4):
            for way in range(2):
                if step > 0:
                    arrival(way, step - 1, piece).wait_recv()
                if travels(way, step, piece):
                    copy(way, step, piece).start()
        if step == 0:
            for item in locals_:
                item.wait()
            todo = [me_index]
        else:
            todo = [at(me - step), at(me + step)]
        for index in todo:
            project(order, index)
            swaps.append((order, index))
            order += 1
    for piece in range(4):
        arrival(piece // 2, steps - 1, piece).wait_recv()
    index = at(me + steps)
    project(order, index)
    swaps.append((order, index))

    for step in range(steps):
        for piece in range(4):
            for way in range(2):
                if travels(way, step, piece):
                    copy(way, step, piece).wait_send()
    for order, index in swaps:
        swap(order, index).wait()

    @pl.loop(0, n)
    def _(block):
        at_rows = pl.ds(pl.multiple_of(block * rows, rows), rows)
        out_ref[at_rows, :] = out_ref[at_rows, :] + other[at_rows, :]


def gather_project(tokens, w_query, w_kv, k_cache, v_cache, n, snake):
    rows, features = tokens.shape
    cols = w_query.shape[1]
    kv_cols = w_kv.shape[1]
    kv_heads, slots, head_size = k_cache.shape
    heads = kv_heads // 2
    pair = heads * head_size
    width = cols // 2 + kv_cols
    any_ = pl.BlockSpec(memory_space=pl.ANY)
    cache = jax.ShapeDtypeStruct((heads, n * slots, head_size), k_cache.dtype)
    return pl.pallas_call(
        functools.partial(gather_kernel, n, snake, pair),
        out_shape=(jax.ShapeDtypeStruct((n * rows, width), jnp.float32), cache, cache),
        in_specs=[any_] * 5,
        out_specs=(pl.BlockSpec(memory_space=pltpu.VMEM), any_, any_),
        scratch_shapes=[
            pltpu.VMEM((n, rows, features), tokens.dtype),
            pltpu.VMEM((features, cols), w_query.dtype),
            pltpu.VMEM((features, kv_cols), w_kv.dtype),
            pltpu.VMEM((n * rows, width), jnp.float32),
            pltpu.VMEM((n * rows, width), jnp.float32),
            pltpu.SemaphoreType.DMA((6,)),
            pltpu.SemaphoreType.DMA((2, n // 2, 4)),
            pltpu.SemaphoreType.DMA((2, n // 2, 4)),
            pltpu.SemaphoreType.DMA((n,)),
            pltpu.SemaphoreType.DMA((n,)),
        ],
        compiler_params=pltpu.CompilerParams(
            collective_id=0, has_side_effects=True, vmem_limit_bytes=VMEM_BYTES
        ),
        name="gather_project",
    )(tokens, w_query, w_kv, k_cache, v_cache)


def attend_kernel(scale, start_ref, q_ref, kc_ref, vc_ref, nk_ref, nv_ref, out_ref):
    block = q_ref.shape[1]
    query = q_ref[0]
    contract = (((1,), (1,)), ((), ()))
    start = start_ref[0]
    old = lax.dot_general(query, kc_ref[0], contract, preferred_element_type=jnp.float32)
    new = lax.dot_general(query, nk_ref[0], contract, preferred_element_type=jnp.float32)
    slot = lax.broadcasted_iota(jnp.int32, old.shape, 1)
    old = jnp.where(slot < start, old, -jnp.inf)
    row = lax.broadcasted_iota(jnp.int32, new.shape, 0) + pl.program_id(1) * block
    col = lax.broadcasted_iota(jnp.int32, new.shape, 1)
    new = jnp.where(col <= row, new, -jnp.inf)
    peak = jnp.maximum(
        jnp.max(old, -1, keepdims=True), jnp.max(new, -1, keepdims=True)
    )
    old = jnp.exp((old - peak) * scale)
    new = jnp.exp((new - peak) * scale)
    total = jnp.sum(old, -1, keepdims=True) + jnp.sum(new, -1, keepdims=True)
    weighted = jnp.dot(
        old.astype(jnp.bfloat16), vc_ref[0], preferred_element_type=jnp.float32
    ) + jnp.dot(new.astype(jnp.bfloat16), nv_ref[0], preferred_element_type=jnp.float32)
    out_ref[...] = (weighted / total).astype(out_ref.dtype)


def attend(start, queries, old_keys, old_values, new_keys, new_values):
    heads, span, head_size = queries.shape
    groups, slots, _ = old_keys.shape
    block = 256
    old = pl.BlockSpec((1, slots, head_size), lambda h, q: (h % groups, 0, 0))
    new = pl.BlockSpec((1, span, head_size), lambda h, q: (h % groups, 0, 0))
    return pl.pallas_call(
        functools.partial(attend_kernel, head_size ** (-0.5)),
        grid=(heads, span // block),
        out_shape=jax.ShapeDtypeStruct((span, heads * head_size), jnp.bfloat16),
        in_specs=[
            pl.BlockSpec(memory_space=pltpu.SMEM),
            pl.BlockSpec((1, block, head_size), lambda h, q: (h, q, 0)),
            old, old, new, new,
        ],
        out_specs=pl.BlockSpec((block, head_size), lambda h, q: (q, h)),
        compiler_params=pltpu.CompilerParams(vmem_limit_bytes=VMEM_BYTES),
        name="attend",
    )(start, queries, old_keys, old_values, new_keys, new_values)


def scatter_kernel(
    n, snake, pair,
    h_ref, w_hbm, out_ref,
    merged, w, sums, own,
    local_sem, send_sem, recv_sem, pair_send, pair_recv,
):
    core = lax.axis_index("dout")
    me_index = lax.axis_index("din")
    me = ring_place(me_index, n, snake)
    at = lambda pos: ring_index(lax.rem(pos + 2 * n, n), n, snake)
    right, left = at(me + 1), at(me - 1)
    rows, width = out_ref.shape
    half = rows // 2
    steps = n // 2
    pairs = h_ref.shape[1] // pair
    tile = 512

    weights = pltpu.make_async_copy(w_hbm, w, local_sem.at[pairs])
    weights.start()
    enter(right, left, core)
    swaps, keeps = [], []
    for m in range(pairs):
        source = h_ref.at[:, pl.ds(m * pair, pair)]
        to = merged.at[:, pl.ds(pl.multiple_of((2 * m + core) * pair, pair), pair)]
        theirs = merged.at[:, pl.ds(pl.multiple_of((2 * m + 1 - core) * pair, pair), pair)]
        keeps.append(pltpu.make_async_copy(source, to, local_sem.at[m]))
        keeps[-1].start()
        pltpu.make_async_remote_copy(
            src_ref=source, dst_ref=to,
            send_sem=pair_send.at[m], recv_sem=pair_recv.at[m],
            device_id={"dout": 1 - core}, device_id_type=MESH,
        ).start()
        swaps.append(
            pltpu.make_async_remote_copy(
                src_ref=source, dst_ref=theirs,
                send_sem=pair_send.at[m], recv_sem=pair_recv.at[m],
                device_id={"dout": 1 - core}, device_id_type=MESH,
            )
        )

    part_rows = [pl.ds(0, half), pl.ds(half, half)]

    def multiply(way, index):
        source = pl.ds(pl.multiple_of(index * rows, rows), rows)

        @pl.loop(0, width // tile)
        def _(j):
            to = pl.ds(pl.multiple_of(j * tile, tile), tile)
            own[way, :, to] = jnp.dot(
                merged[source, :], w[:, to], preferred_element_type=jnp.float32
            )

    def copy(way, step, piece):
        return pltpu.make_async_remote_copy(
            src_ref=sums.at[way, step, part_rows[piece]],
            dst_ref=sums.at[way, step + 1, part_rows[piece]],
            send_sem=send_sem.at[way, step, piece],
            recv_sem=recv_sem.at[way, step, piece],
            device_id={"din": right if way == 0 else left},
            device_id_type=MESH,
        )

    def travels(way, step, piece):
        return step > 0 or piece == way

    for item in keeps:
        item.wait()
    for item in swaps:
        item.wait()
    weights.wait()

    for step in range(steps):
        if step == 0:
            multiply(0, at(me + steps))
        for piece in range(2):
            for way in range(2):
                if not travels(way, step, piece):
                    continue
                source = own.at[0 if step == 0 else way]
                if step > 0 and travels(way, step - 1, piece):
                    copy(way, step - 1, piece).wait_recv()
                    sums[way, step, part_rows[piece]] = (
                        sums[way, step, part_rows[piece]].astype(jnp.float32)
                        + source[part_rows[piece]]
                    ).astype(sums.dtype)
                else:
                    sums[way, step, part_rows[piece]] = source[part_rows[piece]].astype(sums.dtype)
                copy(way, step, piece).start()
        if step < steps - 1:
            multiply(0, at(me + steps - step - 1))
            multiply(1, at(me - (steps - step - 1)))
        else:
            multiply(0, me_index)
    for piece in range(2):
        for way in range(2):
            copy(way, steps - 1, piece).wait_recv()
        block = part_rows[piece]
        out_ref[block] = (
            own[0, block]
            + sums[0, steps, block].astype(jnp.float32)
            + sums[1, steps, block].astype(jnp.float32)
        ).astype(out_ref.dtype)
    for step in range(steps):
        for piece in range(2):
            for way in range(2):
                if travels(way, step, piece):
                    copy(way, step, piece).wait_send()


def project_scatter(heads_out, w_out, pair, n, snake):
    span, own_cols = heads_out.shape
    cols, width = w_out.shape
    rows = span // n
    any_ = pl.BlockSpec(memory_space=pl.ANY)
    pairs = own_cols // pair
    return pl.pallas_call(
        functools.partial(scatter_kernel, n, snake, pair),
        out_shape=jax.ShapeDtypeStruct((rows, width), jnp.bfloat16),
        in_specs=[any_, any_],
        out_specs=pl.BlockSpec(memory_space=pltpu.VMEM),
        scratch_shapes=[
            pltpu.VMEM((span, cols), jnp.bfloat16),
            pltpu.VMEM((cols, width), w_out.dtype),
            pltpu.VMEM((2, n // 2 + 1, rows, width), jnp.bfloat16),
            pltpu.VMEM((2, rows, width), jnp.float32),
            pltpu.SemaphoreType.DMA((pairs + 1,)),
            pltpu.SemaphoreType.DMA((2, n // 2, 2)),
            pltpu.SemaphoreType.DMA((2, n // 2, 2)),
            pltpu.SemaphoreType.DMA((pairs,)),
            pltpu.SemaphoreType.DMA((pairs,)),
        ],
        compiler_params=pltpu.CompilerParams(
            collective_id=1, has_side_effects=True, vmem_limit_bytes=VMEM_BYTES
        ),
        name="project_scatter",
    )(heads_out, w_out)


def local(n, snake, tokens, w_query, w_key, w_value, w_out, k_cache, v_cache, span_start):
    kv_heads, _, head_size = k_cache.shape
    core = lax.axis_index("dout")
    heads = kv_heads // 2
    pair = heads * head_size
    own_cols = w_query.shape[1] // 2
    key_cols = w_key.shape[1]
    span = n * tokens.shape[0]
    cosine, sine = rope_tables(span_start[0] + jnp.arange(span, dtype=jnp.int32), head_size)
    w_kv = jnp.concatenate([w_key, w_value], 1)
    sums, old_keys, old_values = gather_project(
        tokens, w_query, w_kv, k_cache, v_cache, n, snake
    )
    kv = lax.all_gather(sums[:, own_cols:].astype(jnp.bfloat16), "din", axis=0)
    queries = sums[:, :own_cols].reshape(span, own_cols // head_size, head_size)
    queries = rotate(queries.transpose(1, 0, 2), cosine, sine).astype(jnp.bfloat16)

    def mine(block):
        whole = block.reshape(2, n // 2, span, key_cols)
        part = lax.dynamic_index_in_dim(whole, core, 0, keepdims=False)
        part = part.transpose(1, 0, 2).reshape(span, heads, head_size)
        return part.transpose(1, 0, 2)

    new_keys = rotate(mine(kv[:, :, :key_cols]).astype(jnp.float32), cosine, sine).astype(
        jnp.bfloat16
    )
    new_values = mine(kv[:, :, key_cols:])
    heads_out = attend(span_start, queries, old_keys, old_values, new_keys, new_values)
    return project_scatter(heads_out, w_out, pair, n, snake)


def solution(mesh):
    n = mesh.shape["din"]
    snake = n == 8
    return jax.shard_map(
        functools.partial(local, n, snake),
        mesh=mesh,
        in_specs=(
            P(("groups", "din"), "dout"),
            P("dout", "din"),
            P("dout", "din"),
            P("dout", "din"),
            P("din", "dout"),
            P("groups", "din", None),
            P("groups", "din", None),
            P("groups"),
        ),
        out_specs=P(("groups", "din"), "dout"),
        check_vma=False,
    )
```

```python
import functools
import math

import jax
import jax.numpy as jnp
from jax import lax
from jax.experimental import pallas as pl
from jax.experimental.pallas import tpu as pltpu
from jax.sharding import PartitionSpec as P

rope_base = 500000.0
MESH = pl.DeviceIdType.MESH
VMEM_BYTES = 60 * 2**20


def ring_index(pos, n, snake):
    if not snake:
        return pos
    high = pos // (n // 2)
    return (1 - high) * 2 * pos + high * (2 * (n - 1 - pos) + 1)


def ring_place(index, n, snake):
    if not snake:
        return index
    odd = index % 2
    return (1 - odd) * (index // 2) + odd * (n - 1 - index // 2)


def enter(right, left, core):
    barrier = pltpu.get_barrier_semaphore()
    for target in ({"din": right}, {"din": left}, {"dout": 1 - core}):
        pl.semaphore_signal(barrier, inc=1, device_id=target, device_id_type=MESH)
    pl.semaphore_wait(barrier, 3)


def rope_tables(positions, head_size):
    half = head_size // 2
    freq = jnp.exp(
        jnp.arange(half, dtype=jnp.float32) * (-2.0 * math.log(rope_base) / head_size)
    )
    angle = positions.astype(jnp.float32)[:, None] * freq[None, :]
    cosine, sine = jnp.cos(angle), jnp.sin(angle)
    return jnp.concatenate([cosine, cosine], 1), jnp.concatenate([-sine, sine], 1)


def turn(values, cosine, sine):
    return values * cosine + pltpu.roll(values, values.shape[1] // 2, 1) * sine


def gather_kernel(
    n, snake, pair,
    x_ref, wq_hbm, wk_hbm, wv_hbm, k_ref, v_ref, cos_ref, sin_ref,
    q_ref, kv_ref, kc_ref, vc_ref,
    buf, wq, wkv, out_ref, part, other, kvbuf,
    local_sem, send_sem, recv_sem, pair_send, pair_recv, kv_send, kv_recv, end_sem,
):
    core = lax.axis_index("dout")
    me_index = lax.axis_index("din")
    me = ring_place(me_index, n, snake)
    at = lambda pos: ring_index(lax.rem(pos + 2 * n, n), n, snake)
    right, left = at(me + 1), at(me - 1)
    rows = x_ref.shape[0]
    half = rows // 2
    slots = k_ref.shape[1]
    heads = kc_ref.shape[0]
    cols = wq.shape[1]
    own_cols = cols // 2
    key_cols = wk_hbm.shape[0]
    span = n * rows
    steps = n // 2

    mine_heads = pl.ds(core * heads, heads)
    first = [
        x_ref.at[pl.ds(0, half)],
        k_ref.at[mine_heads],
        x_ref.at[pl.ds(half, half)],
        v_ref.at[mine_heads],
    ]

    def place(index, piece):
        if piece == 0:
            return buf.at[index, pl.ds(0, half)]
        if piece == 2:
            return buf.at[index, pl.ds(half, half)]
        ref = kc_ref if piece == 1 else vc_ref
        return ref.at[:, pl.ds(pl.multiple_of(index * slots, slots), slots)]

    locals_ = [
        pltpu.make_async_copy(first[piece], place(me_index, piece), local_sem.at[piece])
        for piece in range(4)
    ] + [
        pltpu.make_async_copy(wq_hbm, wq, local_sem.at[4]),
        pltpu.make_async_copy(wk_hbm, wkv.at[pl.ds(0, key_cols)], local_sem.at[5]),
        pltpu.make_async_copy(wv_hbm, wkv.at[pl.ds(key_cols, key_cols)], local_sem.at[6]),
    ]

    def copy(way, step, piece):
        index = at(me - step if way == 0 else me + step)
        return pltpu.make_async_remote_copy(
            src_ref=first[piece] if step == 0 else place(index, piece),
            dst_ref=place(index, piece),
            send_sem=send_sem.at[way, step, piece],
            recv_sem=recv_sem.at[way, step, piece],
            device_id={"din": right if way == 0 else left},
            device_id_type=MESH,
        )

    def arrival(way, step, piece):
        index = at(me - 1 - step if way == 0 else me + 1 + step)
        return pltpu.make_async_remote_copy(
            src_ref=place(index, piece),
            dst_ref=place(index, piece),
            send_sem=send_sem.at[way, step, piece],
            recv_sem=recv_sem.at[way, step, piece],
            device_id={"din": right if way == 0 else left},
            device_id_type=MESH,
        )

    def travels(way, step, piece):
        return step < steps - 1 or (piece // 2 == way)

    def swap(order, index):
        at_rows = pl.ds(pl.multiple_of(index * rows, rows), rows)
        return pltpu.make_async_remote_copy(
            src_ref=part.at[at_rows],
            dst_ref=other.at[at_rows],
            send_sem=pair_send.at[order],
            recv_sem=pair_recv.at[order],
            device_id={"dout": 1 - core},
            device_id_type=MESH,
        )

    def project(order, index):
        at_rows = pl.ds(pl.multiple_of(index * rows, rows), rows)

        @pl.loop(0, own_cols // pair)
        def _(m):
            to = pl.ds(pl.multiple_of(m * pair, pair), pair)
            mine = pl.ds(pl.multiple_of((2 * m + core) * pair, pair), pair)
            theirs = pl.ds(pl.multiple_of((2 * m + 1 - core) * pair, pair), pair)
            part[at_rows, to] = jnp.dot(
                buf[index], wq[:, theirs], preferred_element_type=jnp.float32
            )
            out_ref[at_rows, to] = jnp.dot(
                buf[index], wq[:, mine], preferred_element_type=jnp.float32
            )

        both = lax.dot_general(
            buf[index], wkv[...], (((1,), (1,)), ((), ())), preferred_element_type=jnp.float32
        )
        part[at_rows, own_cols:] = both
        out_ref[at_rows, own_cols:] = both
        swap(order, index).start()

    def finish(order, index):
        swap(order, index).wait()
        at_rows = pl.ds(pl.multiple_of(index * rows, rows), rows)
        cosine, sine = cos_ref[at_rows, :], sin_ref[at_rows, :]
        size = cosine.shape[1]
        for head in range(own_cols // size):
            to = slice(head * size, (head + 1) * size)
            value = out_ref[at_rows, to] + other[at_rows, to]
            q_ref[at_rows, to] = turn(value, cosine, sine).astype(q_ref.dtype)

        @pl.when(index // steps == core)
        def _():
            kvbuf[me_index, at_rows, :] = (
                out_ref[at_rows, own_cols:] + other[at_rows, own_cols:]
            ).astype(kvbuf.dtype)

    def kv_place(pos, piece):
        quarter = span // 4
        first_row = pl.multiple_of(core * 2 * quarter + piece * quarter, quarter)
        return kvbuf.at[at(pos), pl.ds(first_row, quarter)]

    def kv_copy(way, step, piece, arriving=False):
        back = step + 1 if arriving else step
        block = kv_place(me - back if way == 0 else me + back, piece)
        return pltpu.make_async_remote_copy(
            src_ref=block,
            dst_ref=block,
            send_sem=kv_send.at[way, step, piece],
            recv_sem=kv_recv.at[way, step, piece],
            device_id={"din": right if way == 0 else left},
            device_id_type=MESH,
        )

    for item in locals_:
        item.start()
    enter(right, left, core)

    order = 0
    swaps = []
    for step in range(steps):
        for piece in range(4):
            for way in range(2):
                if step > 0:
                    arrival(way, step - 1, piece).wait_recv()
                if travels(way, step, piece):
                    copy(way, step, piece).start()
        if step == 0:
            for item in locals_:
                item.wait()
            todo = [me_index]
        else:
            todo = [at(me - step), at(me + step)]
        fresh = []
        for index in todo:
            project(order, index)
            fresh.append((order, index))
            order += 1
        for item in swaps:
            finish(*item)
        swaps = fresh
    for item in swaps:
        finish(*item)
    for piece in range(4):
        arrival(piece // 2, steps - 1, piece).wait_recv()
    index = at(me + steps)
    project(order, index)
    finish(order, index)

    for step in range(steps):
        for piece in range(2):
            for way in range(2):
                if step > 0:
                    kv_copy(way, step - 1, piece, True).wait_recv()
                if step < steps - 1 or piece == way:
                    kv_copy(way, step, piece).start()
    for piece in range(2):
        kv_copy(piece, steps - 1, piece, True).wait_recv()

    mine_rows = pl.ds(pl.multiple_of(core * (span // 2), span // 2), span // 2)
    their_rows = pl.ds(pl.multiple_of((1 - core) * (span // 2), span // 2), span // 2)
    outgoing = kvbuf.at[pl.ds((1 - core) * steps, steps), mine_rows]
    incoming = kvbuf.at[pl.ds(core * steps, steps), their_rows]
    send = pltpu.make_async_remote_copy(
        src_ref=outgoing, dst_ref=outgoing,
        send_sem=pair_send.at[n], recv_sem=pair_recv.at[n],
        device_id={"dout": 1 - core}, device_id_type=MESH,
    )
    receive = pltpu.make_async_remote_copy(
        src_ref=incoming, dst_ref=incoming,
        send_sem=pair_send.at[n], recv_sem=pair_recv.at[n],
        device_id={"dout": 1 - core}, device_id_type=MESH,
    )
    send.start()
    for step in range(steps):
        for piece in range(4):
            for way in range(2):
                if travels(way, step, piece):
                    copy(way, step, piece).wait_send()
        for piece in range(2):
            for way in range(2):
                if step < steps - 1 or piece == way:
                    kv_copy(way, step, piece).wait_send()
    send.wait_send()
    receive.wait_recv()
    last = pltpu.make_async_copy(kvbuf.at[pl.ds(core * steps, steps)], kv_ref, end_sem.at[0])
    last.start()
    last.wait()


def gather_project(tokens, w_query, w_key, w_value, k_cache, v_cache, cosine, sine, n, snake):
    rows, features = tokens.shape
    cols = w_query.shape[1]
    kv_cols = 2 * w_key.shape[0]
    kv_heads, slots, head_size = k_cache.shape
    heads = kv_heads // 2
    pair = heads * head_size
    width = cols // 2 + kv_cols
    span = n * rows
    any_ = pl.BlockSpec(memory_space=pl.ANY)
    vmem = pl.BlockSpec(memory_space=pltpu.VMEM)
    cache = jax.ShapeDtypeStruct((heads, n * slots, head_size), k_cache.dtype)
    return pl.pallas_call(
        functools.partial(gather_kernel, n, snake, pair),
        out_shape=(
            jax.ShapeDtypeStruct((span, cols // 2), jnp.bfloat16),
            jax.ShapeDtypeStruct((n // 2, span, kv_cols), jnp.bfloat16),
            cache,
            cache,
        ),
        in_specs=[any_] * 6 + [vmem] * 2,
        out_specs=(vmem, any_, any_, any_),
        scratch_shapes=[
            pltpu.VMEM((n, rows, features), tokens.dtype),
            pltpu.VMEM((features, cols), w_query.dtype),
            pltpu.VMEM((kv_cols, features), w_key.dtype),
            pltpu.VMEM((span, width), jnp.float32),
            pltpu.VMEM((span, width), jnp.float32),
            pltpu.VMEM((span, width), jnp.float32),
            pltpu.VMEM((n, span, kv_cols), jnp.bfloat16),
            pltpu.SemaphoreType.DMA((7,)),
            pltpu.SemaphoreType.DMA((2, n // 2, 4)),
            pltpu.SemaphoreType.DMA((2, n // 2, 4)),
            pltpu.SemaphoreType.DMA((n + 1,)),
            pltpu.SemaphoreType.DMA((n + 1,)),
            pltpu.SemaphoreType.DMA((2, n // 2, 2)),
            pltpu.SemaphoreType.DMA((2, n // 2, 2)),
            pltpu.SemaphoreType.DMA((1,)),
        ],
        compiler_params=pltpu.CompilerParams(
            collective_id=0, has_side_effects=True, vmem_limit_bytes=VMEM_BYTES
        ),
        name="gather_project",
    )(tokens, w_query, w_key, w_value, k_cache, v_cache, cosine, sine)


def scatter_kernel(
    n, snake, pair,
    start_ref, q_ref, kv_ref, kc_ref, vc_ref, cos_ref, sin_ref, w_hbm, out_ref,
    merged, w, sums, own, nk, nv,
    local_sem, send_sem, recv_sem, pair_send, pair_recv,
):
    core = lax.axis_index("dout")
    me_index = lax.axis_index("din")
    me = ring_place(me_index, n, snake)
    at = lambda pos: ring_index(lax.rem(pos + 2 * n, n), n, snake)
    right, left = at(me + 1), at(me - 1)
    rows, width = out_ref.shape
    half = rows // 2
    steps = n // 2
    pairs = q_ref.shape[1] // pair
    tile = 512
    heads, span, size = nk.shape
    key_cols = kv_ref.shape[2] // 2
    per = size // key_cols
    scale = size ** (-0.5)
    start_pos = start_ref[0]
    contract = (((1,), (1,)), ((), ()))

    weights = pltpu.make_async_copy(w_hbm, w, local_sem.at[0])
    weights.start()
    enter(right, left, core)
    for head in range(heads):
        blocks = [kv_ref[head * per + item] for item in range(per)]
        key = jnp.concatenate([block[:, :key_cols].astype(jnp.float32) for block in blocks], 1)
        value = jnp.concatenate([block[:, key_cols:].astype(jnp.float32) for block in blocks], 1)
        nk[head] = turn(key, cos_ref[...], sin_ref[...]).astype(nk.dtype)
        nv[head] = value.astype(nv.dtype)

    def swap(order, m, index, owner):
        block = merged.at[
            pl.ds(pl.multiple_of(index * rows, rows), rows),
            pl.ds(pl.multiple_of((2 * m + owner) * pair, pair), pair),
        ]
        return pltpu.make_async_remote_copy(
            src_ref=block, dst_ref=block,
            send_sem=pair_send.at[order, m], recv_sem=pair_recv.at[order, m],
            device_id={"dout": 1 - core}, device_id_type=MESH,
        )

    def attend(order, index):
        at_rows = pl.ds(pl.multiple_of(index * rows, rows), rows)
        for m in range(pairs):
            for head in range(heads):
                query = q_ref[at_rows, m * pair + head * size : m * pair + (head + 1) * size]
                old = lax.dot_general(
                    query, kc_ref[head], contract, preferred_element_type=jnp.float32
                )
                new = lax.dot_general(
                    query, nk[head], contract, preferred_element_type=jnp.float32
                )
                slot = lax.broadcasted_iota(jnp.int32, old.shape, 1)
                old = jnp.where(slot < start_pos, old, -jnp.inf)
                row = lax.broadcasted_iota(jnp.int32, new.shape, 0) + index * rows
                col = lax.broadcasted_iota(jnp.int32, new.shape, 1)
                new = jnp.where(col <= row, new, -jnp.inf)
                peak = jnp.maximum(
                    jnp.max(old, -1, keepdims=True), jnp.max(new, -1, keepdims=True)
                )
                old = jnp.exp((old - peak) * scale)
                new = jnp.exp((new - peak) * scale)
                total = jnp.sum(old, -1, keepdims=True) + jnp.sum(new, -1, keepdims=True)
                weighted = jnp.dot(
                    old.astype(jnp.bfloat16), vc_ref[head], preferred_element_type=jnp.float32
                ) + jnp.dot(new.astype(jnp.bfloat16), nv[head], preferred_element_type=jnp.float32)
                to = pl.multiple_of((2 * m + core) * pair + head * size, size)
                merged[at_rows, pl.ds(to, size)] = (weighted / total).astype(merged.dtype)
            swap(order, m, index, core).start()

    def joined(order, index):
        for m in range(pairs):
            swap(order, m, index, core).wait_send()
            swap(order, m, index, 1 - core).wait_recv()

    part_rows = [pl.ds(0, half), pl.ds(half, half)]

    def multiply(way, index):
        source = pl.ds(pl.multiple_of(index * rows, rows), rows)

        @pl.loop(0, width // tile)
        def _(j):
            to = pl.ds(pl.multiple_of(j * tile, tile), tile)
            own[way, :, to] = jnp.dot(
                merged[source, :], w[:, to], preferred_element_type=jnp.float32
            )

    def copy(way, step, piece):
        return pltpu.make_async_remote_copy(
            src_ref=sums.at[way, step, part_rows[piece]],
            dst_ref=sums.at[way, step + 1, part_rows[piece]],
            send_sem=send_sem.at[way, step, piece],
            recv_sem=recv_sem.at[way, step, piece],
            device_id={"din": right if way == 0 else left},
            device_id_type=MESH,
        )

    def travels(way, step, piece):
        return step > 0 or piece == way

    for step in range(steps):
        if step == 0:
            attend(0, at(me + steps))
            weights.wait()
            joined(0, at(me + steps))
            multiply(0, at(me + steps))
        for piece in range(2):
            for way in range(2):
                if not travels(way, step, piece):
                    continue
                source = own.at[0 if step == 0 else way]
                if step > 0 and travels(way, step - 1, piece):
                    copy(way, step - 1, piece).wait_recv()
                    sums[way, step, part_rows[piece]] = (
                        sums[way, step, part_rows[piece]].astype(jnp.float32)
                        + source[part_rows[piece]]
                    ).astype(sums.dtype)
                else:
                    sums[way, step, part_rows[piece]] = source[part_rows[piece]].astype(sums.dtype)
                copy(way, step, piece).start()
        if step < steps - 1:
            todo = [at(me + steps - step - 1), at(me - (steps - step - 1))]
        else:
            todo = [me_index]
        for way, index in enumerate(todo):
            attend(2 * step + 1 + way, index)
        for way, index in enumerate(todo):
            joined(2 * step + 1 + way, index)
            multiply(way, index)
    for piece in range(2):
        for way in range(2):
            copy(way, steps - 1, piece).wait_recv()
        block = part_rows[piece]
        out_ref[block] = (
            own[0, block]
            + sums[0, steps, block].astype(jnp.float32)
            + sums[1, steps, block].astype(jnp.float32)
        ).astype(out_ref.dtype)
    for step in range(steps):
        for piece in range(2):
            for way in range(2):
                if travels(way, step, piece):
                    copy(way, step, piece).wait_send()


def attend_scatter(start, queries, kv, k_old, v_old, cosine, sine, w_out, n, snake):
    span, own_cols = queries.shape
    cols, width = w_out.shape
    rows = span // n
    heads, _, size = k_old.shape
    pair = heads * size
    pairs = own_cols // pair
    vmem = pl.BlockSpec(memory_space=pltpu.VMEM)
    return pl.pallas_call(
        functools.partial(scatter_kernel, n, snake, pair),
        out_shape=jax.ShapeDtypeStruct((rows, width), jnp.bfloat16),
        in_specs=[pl.BlockSpec(memory_space=pltpu.SMEM)]
        + [vmem] * 6
        + [pl.BlockSpec(memory_space=pl.ANY)],
        out_specs=vmem,
        scratch_shapes=[
            pltpu.VMEM((span, cols), jnp.bfloat16),
            pltpu.VMEM((cols, width), w_out.dtype),
            pltpu.VMEM((2, n // 2 + 1, rows, width), jnp.bfloat16),
            pltpu.VMEM((2, rows, width), jnp.float32),
            pltpu.VMEM((heads, span, size), jnp.bfloat16),
            pltpu.VMEM((heads, span, size), jnp.bfloat16),
            pltpu.SemaphoreType.DMA((1,)),
            pltpu.SemaphoreType.DMA((2, n // 2, 2)),
            pltpu.SemaphoreType.DMA((2, n // 2, 2)),
            pltpu.SemaphoreType.DMA((n, pairs)),
            pltpu.SemaphoreType.DMA((n, pairs)),
        ],
        compiler_params=pltpu.CompilerParams(
            collective_id=1, has_side_effects=True, vmem_limit_bytes=VMEM_BYTES
        ),
        name="attend_scatter",
    )(start, queries, kv, k_old, v_old, cosine, sine, w_out)


def local(n, snake, tokens, w_query, w_key, w_value, w_out, k_cache, v_cache, span_start):
    span = n * tokens.shape[0]
    positions = span_start[0] + jnp.arange(span, dtype=jnp.int32)
    cosine, sine = rope_tables(positions, k_cache.shape[2])
    queries, kv, k_old, v_old = gather_project(
        tokens, w_query, w_key.T, w_value.T, k_cache, v_cache, cosine, sine, n, snake
    )
    return attend_scatter(
        span_start, queries, kv, k_old, v_old, cosine, sine, w_out, n, snake
    )


def solution(mesh):
    n = mesh.shape["din"]
    snake = n == 8
    return jax.shard_map(
        functools.partial(local, n, snake),
        mesh=mesh,
        in_specs=(
            P(("groups", "din"), "dout"),
            P("dout", "din"),
            P("dout", "din"),
            P("dout", "din"),
            P("din", "dout"),
            P("groups", "din", None),
            P("groups", "din", None),
            P("groups"),
        ),
        out_specs=P(("groups", "din"), "dout"),
        check_vma=False,
    )
```

```python
import functools
import math

import jax
import jax.numpy as jnp
from jax import lax
from jax.experimental import pallas as pl
from jax.experimental.pallas import tpu as pltpu
from jax.sharding import PartitionSpec as P

rope_base = 500000.0
MESH = pl.DeviceIdType.MESH
VMEM_BYTES = 60 * 2**20


def ring_index(pos, n, snake):
    if not snake:
        return pos
    high = pos // (n // 2)
    return (1 - high) * 2 * pos + high * (2 * (n - 1 - pos) + 1)


def ring_place(index, n, snake):
    if not snake:
        return index
    odd = index % 2
    return (1 - odd) * (index // 2) + odd * (n - 1 - index // 2)


def enter(right, left, core):
    barrier = pltpu.get_barrier_semaphore()
    for target in ({"din": right}, {"din": left}, {"dout": 1 - core}):
        pl.semaphore_signal(barrier, inc=1, device_id=target, device_id_type=MESH)
    pl.semaphore_wait(barrier, 3)


def rope_tables(positions, head_size):
    half = head_size // 2
    freq = jnp.exp(
        jnp.arange(half, dtype=jnp.float32) * (-2.0 * math.log(rope_base) / head_size)
    )
    angle = positions.astype(jnp.float32)[:, None] * freq[None, :]
    cosine, sine = jnp.cos(angle), jnp.sin(angle)
    return jnp.concatenate([cosine, cosine], 1), jnp.concatenate([-sine, sine], 1)


def turn(values, cosine, sine):
    return values * cosine + pltpu.roll(values, values.shape[1] // 2, 1) * sine


def gather_kernel(
    n, snake, pair,
    x_ref, wq_hbm, wk_hbm, wv_hbm, k_ref, v_ref, cos_ref, sin_ref,
    q_ref, kv_ref, kc_ref, vc_ref,
    buf, wq, wkv, out_ref, part, other, kvbuf,
    local_sem, send_sem, recv_sem, pair_send, pair_recv, kv_send, kv_recv, end_sem,
):
    core = lax.axis_index("dout")
    me_index = lax.axis_index("din")
    me = ring_place(me_index, n, snake)
    at = lambda pos: ring_index(lax.rem(pos + 2 * n, n), n, snake)
    right, left = at(me + 1), at(me - 1)
    rows = x_ref.shape[0]
    half = rows // 2
    slots = k_ref.shape[1]
    heads = kc_ref.shape[0]
    cols = wq.shape[1]
    own_cols = cols // 2
    key_cols = wk_hbm.shape[0]
    span = n * rows
    steps = n // 2

    mine_heads = pl.ds(core * heads, heads)
    first = [
        x_ref.at[pl.ds(0, half)],
        k_ref.at[mine_heads],
        x_ref.at[pl.ds(half, half)],
        v_ref.at[mine_heads],
    ]

    def place(index, piece):
        if piece == 0:
            return buf.at[index, pl.ds(0, half)]
        if piece == 2:
            return buf.at[index, pl.ds(half, half)]
        ref = kc_ref if piece == 1 else vc_ref
        return ref.at[:, pl.ds(pl.multiple_of(index * slots, slots), slots)]

    locals_ = [
        pltpu.make_async_copy(first[piece], place(me_index, piece), local_sem.at[piece])
        for piece in range(4)
    ] + [
        pltpu.make_async_copy(wq_hbm, wq, local_sem.at[4]),
        pltpu.make_async_copy(wk_hbm, wkv.at[pl.ds(0, key_cols)], local_sem.at[5]),
        pltpu.make_async_copy(wv_hbm, wkv.at[pl.ds(key_cols, key_cols)], local_sem.at[6]),
    ]

    def copy(way, step, piece):
        index = at(me - step if way == 0 else me + step)
        return pltpu.make_async_remote_copy(
            src_ref=first[piece] if step == 0 else place(index, piece),
            dst_ref=place(index, piece),
            send_sem=send_sem.at[way, step, piece],
            recv_sem=recv_sem.at[way, step, piece],
            device_id={"din": right if way == 0 else left},
            device_id_type=MESH,
        )

    def arrival(way, step, piece):
        index = at(me - 1 - step if way == 0 else me + 1 + step)
        return pltpu.make_async_remote_copy(
            src_ref=place(index, piece),
            dst_ref=place(index, piece),
            send_sem=send_sem.at[way, step, piece],
            recv_sem=recv_sem.at[way, step, piece],
            device_id={"din": right if way == 0 else left},
            device_id_type=MESH,
        )

    def travels(way, step, piece):
        return step < steps - 1 or (piece // 2 == way)

    def swap(order, index):
        at_rows = pl.ds(pl.multiple_of(index * rows, rows), rows)
        return pltpu.make_async_remote_copy(
            src_ref=part.at[at_rows],
            dst_ref=other.at[at_rows],
            send_sem=pair_send.at[order],
            recv_sem=pair_recv.at[order],
            device_id={"dout": 1 - core},
            device_id_type=MESH,
        )

    def project(order, index):
        at_rows = pl.ds(pl.multiple_of(index * rows, rows), rows)

        @pl.loop(0, own_cols // pair)
        def _(m):
            to = pl.ds(pl.multiple_of(m * pair, pair), pair)
            mine = pl.ds(pl.multiple_of((2 * m + core) * pair, pair), pair)
            theirs = pl.ds(pl.multiple_of((2 * m + 1 - core) * pair, pair), pair)
            part[at_rows, to] = jnp.dot(
                buf[index], wq[:, theirs], preferred_element_type=jnp.float32
            )
            out_ref[at_rows, to] = jnp.dot(
                buf[index], wq[:, mine], preferred_element_type=jnp.float32
            )

        both = lax.dot_general(
            buf[index], wkv[...], (((1,), (1,)), ((), ())), preferred_element_type=jnp.float32
        )
        part[at_rows, own_cols:] = both
        out_ref[at_rows, own_cols:] = both
        swap(order, index).start()

    def finish(order, index):
        swap(order, index).wait()
        at_rows = pl.ds(pl.multiple_of(index * rows, rows), rows)
        cosine, sine = cos_ref[at_rows, :], sin_ref[at_rows, :]
        size = cosine.shape[1]
        for head in range(own_cols // size):
            to = slice(head * size, (head + 1) * size)
            value = out_ref[at_rows, to] + other[at_rows, to]
            q_ref[at_rows, to] = turn(value, cosine, sine).astype(q_ref.dtype)

        @pl.when(index // steps == core)
        def _():
            kvbuf[me_index, at_rows, :] = (
                out_ref[at_rows, own_cols:] + other[at_rows, own_cols:]
            ).astype(kvbuf.dtype)

    def kv_place(pos, piece):
        quarter = span // 4
        first_row = pl.multiple_of(core * 2 * quarter + piece * quarter, quarter)
        return kvbuf.at[at(pos), pl.ds(first_row, quarter)]

    def kv_copy(way, step, piece, arriving=False):
        back = step + 1 if arriving else step
        block = kv_place(me - back if way == 0 else me + back, piece)
        return pltpu.make_async_remote_copy(
            src_ref=block,
            dst_ref=block,
            send_sem=kv_send.at[way, step, piece],
            recv_sem=kv_recv.at[way, step, piece],
            device_id={"din": right if way == 0 else left},
            device_id_type=MESH,
        )

    for item in locals_:
        item.start()
    enter(right, left, core)

    def cache_step(step):
        for piece in (1, 3):
            for way in range(2):
                if step > 0:
                    arrival(way, step - 1, piece).wait_recv()
                if travels(way, step, piece):
                    copy(way, step, piece).start()

    order = 0
    swaps = []
    for step in range(steps):
        if step == steps - 1:
            cache_step(0)
        for piece in (0, 2):
            for way in range(2):
                if step > 0:
                    arrival(way, step - 1, piece).wait_recv()
                if travels(way, step, piece):
                    copy(way, step, piece).start()
        if step == 0:
            for item in locals_:
                item.wait()
            todo = [me_index]
        else:
            todo = [at(me - step), at(me + step)]
        fresh = []
        for index in todo:
            project(order, index)
            fresh.append((order, index))
            order += 1
        for item in swaps:
            finish(*item)
        swaps = fresh
    for item in swaps:
        finish(*item)
    for piece in (0, 2):
        arrival(piece // 2, steps - 1, piece).wait_recv()
    cache_step(1)
    index = at(me + steps)
    project(order, index)
    finish(order, index)

    for step in range(steps):
        for piece in range(2):
            for way in range(2):
                if step > 0:
                    kv_copy(way, step - 1, piece, True).wait_recv()
                if step < steps - 1 or piece == way:
                    kv_copy(way, step, piece).start()
        if step + 2 < steps:
            cache_step(step + 2)
    for piece in range(2):
        kv_copy(piece, steps - 1, piece, True).wait_recv()
        arrival(piece, steps - 1, 2 * piece + 1).wait_recv()

    mine_rows = pl.ds(pl.multiple_of(core * (span // 2), span // 2), span // 2)
    their_rows = pl.ds(pl.multiple_of((1 - core) * (span // 2), span // 2), span // 2)
    outgoing = kvbuf.at[pl.ds((1 - core) * steps, steps), mine_rows]
    incoming = kvbuf.at[pl.ds(core * steps, steps), their_rows]
    send = pltpu.make_async_remote_copy(
        src_ref=outgoing, dst_ref=outgoing,
        send_sem=pair_send.at[n], recv_sem=pair_recv.at[n],
        device_id={"dout": 1 - core}, device_id_type=MESH,
    )
    receive = pltpu.make_async_remote_copy(
        src_ref=incoming, dst_ref=incoming,
        send_sem=pair_send.at[n], recv_sem=pair_recv.at[n],
        device_id={"dout": 1 - core}, device_id_type=MESH,
    )
    send.start()
    for step in range(steps):
        for piece in range(4):
            for way in range(2):
                if travels(way, step, piece):
                    copy(way, step, piece).wait_send()
        for piece in range(2):
            for way in range(2):
                if step < steps - 1 or piece == way:
                    kv_copy(way, step, piece).wait_send()
    send.wait_send()
    receive.wait_recv()
    last = pltpu.make_async_copy(kvbuf.at[pl.ds(core * steps, steps)], kv_ref, end_sem.at[0])
    last.start()
    last.wait()


def gather_project(tokens, w_query, w_key, w_value, k_cache, v_cache, cosine, sine, n, snake):
    rows, features = tokens.shape
    cols = w_query.shape[1]
    kv_cols = 2 * w_key.shape[0]
    kv_heads, slots, head_size = k_cache.shape
    heads = kv_heads // 2
    pair = heads * head_size
    width = cols // 2 + kv_cols
    span = n * rows
    any_ = pl.BlockSpec(memory_space=pl.ANY)
    vmem = pl.BlockSpec(memory_space=pltpu.VMEM)
    cache = jax.ShapeDtypeStruct((heads, n * slots, head_size), k_cache.dtype)
    return pl.pallas_call(
        functools.partial(gather_kernel, n, snake, pair),
        out_shape=(
            jax.ShapeDtypeStruct((span, cols // 2), jnp.bfloat16),
            jax.ShapeDtypeStruct((n // 2, span, kv_cols), jnp.bfloat16),
            cache,
            cache,
        ),
        in_specs=[any_] * 6 + [vmem] * 2,
        out_specs=(vmem, any_, any_, any_),
        scratch_shapes=[
            pltpu.VMEM((n, rows, features), tokens.dtype),
            pltpu.VMEM((features, cols), w_query.dtype),
            pltpu.VMEM((kv_cols, features), w_key.dtype),
            pltpu.VMEM((span, width), jnp.float32),
            pltpu.VMEM((span, width), jnp.float32),
            pltpu.VMEM((span, width), jnp.float32),
            pltpu.VMEM((n, span, kv_cols), jnp.bfloat16),
            pltpu.SemaphoreType.DMA((7,)),
            pltpu.SemaphoreType.DMA((2, n // 2, 4)),
            pltpu.SemaphoreType.DMA((2, n // 2, 4)),
            pltpu.SemaphoreType.DMA((n + 1,)),
            pltpu.SemaphoreType.DMA((n + 1,)),
            pltpu.SemaphoreType.DMA((2, n // 2, 2)),
            pltpu.SemaphoreType.DMA((2, n // 2, 2)),
            pltpu.SemaphoreType.DMA((1,)),
        ],
        compiler_params=pltpu.CompilerParams(
            collective_id=0, has_side_effects=True, vmem_limit_bytes=VMEM_BYTES
        ),
        name="gather_project",
    )(tokens, w_query, w_key, w_value, k_cache, v_cache, cosine, sine)


def scatter_kernel(
    n, snake, pair,
    start_ref, q_ref, kv_ref, kc_ref, vc_ref, cos_ref, sin_ref, w_hbm, out_ref,
    merged, w, sums, own, nk, nv,
    local_sem, send_sem, recv_sem, pair_send, pair_recv,
):
    core = lax.axis_index("dout")
    me_index = lax.axis_index("din")
    me = ring_place(me_index, n, snake)
    at = lambda pos: ring_index(lax.rem(pos + 2 * n, n), n, snake)
    right, left = at(me + 1), at(me - 1)
    rows, width = out_ref.shape
    half = rows // 2
    steps = n // 2
    pairs = q_ref.shape[1] // pair
    tile = 512
    heads, span, size = nk.shape
    key_cols = kv_ref.shape[2] // 2
    per = size // key_cols
    scale = size ** (-0.5)
    start_pos = start_ref[0]
    contract = (((1,), (1,)), ((), ()))

    weights = pltpu.make_async_copy(w_hbm, w, local_sem.at[0])
    weights.start()
    enter(right, left, core)
    for head in range(heads):
        blocks = [kv_ref[head * per + item] for item in range(per)]
        key = jnp.concatenate([block[:, :key_cols].astype(jnp.float32) for block in blocks], 1)
        value = jnp.concatenate([block[:, key_cols:].astype(jnp.float32) for block in blocks], 1)
        nk[head] = turn(key, cos_ref[...], sin_ref[...]).astype(nk.dtype)
        nv[head] = value.astype(nv.dtype)

    def swap(order, m, index, owner):
        block = merged.at[
            pl.ds(pl.multiple_of(index * rows, rows), rows),
            pl.ds(pl.multiple_of((2 * m + owner) * pair, pair), pair),
        ]
        return pltpu.make_async_remote_copy(
            src_ref=block, dst_ref=block,
            send_sem=pair_send.at[order, m], recv_sem=pair_recv.at[order, m],
            device_id={"dout": 1 - core}, device_id_type=MESH,
        )

    def attend(order, index):
        at_rows = pl.ds(pl.multiple_of(index * rows, rows), rows)
        for m in range(pairs):
            for head in range(heads):
                query = q_ref[at_rows, m * pair + head * size : m * pair + (head + 1) * size]
                old = lax.dot_general(
                    query, kc_ref[head], contract, preferred_element_type=jnp.float32
                )
                new = lax.dot_general(
                    query, nk[head], contract, preferred_element_type=jnp.float32
                )
                slot = lax.broadcasted_iota(jnp.int32, old.shape, 1)
                old = jnp.where(slot < start_pos, old, -jnp.inf)
                row = lax.broadcasted_iota(jnp.int32, new.shape, 0) + index * rows
                col = lax.broadcasted_iota(jnp.int32, new.shape, 1)
                new = jnp.where(col <= row, new, -jnp.inf)
                peak = jnp.maximum(
                    jnp.max(old, -1, keepdims=True), jnp.max(new, -1, keepdims=True)
                )
                old = jnp.exp((old - peak) * scale)
                new = jnp.exp((new - peak) * scale)
                total = jnp.sum(old, -1, keepdims=True) + jnp.sum(new, -1, keepdims=True)
                weighted = jnp.dot(
                    old.astype(jnp.bfloat16), vc_ref[head], preferred_element_type=jnp.float32
                ) + jnp.dot(new.astype(jnp.bfloat16), nv[head], preferred_element_type=jnp.float32)
                to = pl.multiple_of((2 * m + core) * pair + head * size, size)
                merged[at_rows, pl.ds(to, size)] = (weighted / total).astype(merged.dtype)
            swap(order, m, index, core).start()

    def joined(order, index):
        for m in range(pairs):
            swap(order, m, index, core).wait_send()
            swap(order, m, index, 1 - core).wait_recv()

    part_rows = [pl.ds(0, half), pl.ds(half, half)]

    def multiply(way, index):
        source = pl.ds(pl.multiple_of(index * rows, rows), rows)

        @pl.loop(0, width // tile)
        def _(j):
            to = pl.ds(pl.multiple_of(j * tile, tile), tile)
            own[way, :, to] = jnp.dot(
                merged[source, :], w[:, to], preferred_element_type=jnp.float32
            )

    def copy(way, step, piece):
        return pltpu.make_async_remote_copy(
            src_ref=sums.at[way, step, part_rows[piece]],
            dst_ref=sums.at[way, step + 1, part_rows[piece]],
            send_sem=send_sem.at[way, step, piece],
            recv_sem=recv_sem.at[way, step, piece],
            device_id={"din": right if way == 0 else left},
            device_id_type=MESH,
        )

    def travels(way, step, piece):
        return step > 0 or piece == way

    for step in range(steps):
        if step == 0:
            attend(0, at(me + steps))
            weights.wait()
            joined(0, at(me + steps))
            multiply(0, at(me + steps))
        for piece in range(2):
            for way in range(2):
                if not travels(way, step, piece):
                    continue
                source = own.at[0 if step == 0 else way]
                if step > 0 and travels(way, step - 1, piece):
                    copy(way, step - 1, piece).wait_recv()
                    sums[way, step, part_rows[piece]] = (
                        sums[way, step, part_rows[piece]].astype(jnp.float32)
                        + source[part_rows[piece]]
                    ).astype(sums.dtype)
                else:
                    sums[way, step, part_rows[piece]] = source[part_rows[piece]].astype(sums.dtype)
                copy(way, step, piece).start()
        if step < steps - 1:
            todo = [at(me + steps - step - 1), at(me - (steps - step - 1))]
        else:
            todo = [me_index]
        for way, index in enumerate(todo):
            attend(2 * step + 1 + way, index)
        for way, index in enumerate(todo):
            joined(2 * step + 1 + way, index)
            multiply(way, index)
    for piece in range(2):
        for way in range(2):
            copy(way, steps - 1, piece).wait_recv()
        block = part_rows[piece]
        out_ref[block] = (
            own[0, block]
            + sums[0, steps, block].astype(jnp.float32)
            + sums[1, steps, block].astype(jnp.float32)
        ).astype(out_ref.dtype)
    for step in range(steps):
        for piece in range(2):
            for way in range(2):
                if travels(way, step, piece):
                    copy(way, step, piece).wait_send()


def attend_scatter(start, queries, kv, k_old, v_old, cosine, sine, w_out, n, snake):
    span, own_cols = queries.shape
    cols, width = w_out.shape
    rows = span // n
    heads, _, size = k_old.shape
    pair = heads * size
    pairs = own_cols // pair
    vmem = pl.BlockSpec(memory_space=pltpu.VMEM)
    return pl.pallas_call(
        functools.partial(scatter_kernel, n, snake, pair),
        out_shape=jax.ShapeDtypeStruct((rows, width), jnp.bfloat16),
        in_specs=[pl.BlockSpec(memory_space=pltpu.SMEM)]
        + [vmem] * 6
        + [pl.BlockSpec(memory_space=pl.ANY)],
        out_specs=vmem,
        scratch_shapes=[
            pltpu.VMEM((span, cols), jnp.bfloat16),
            pltpu.VMEM((cols, width), w_out.dtype),
            pltpu.VMEM((2, n // 2 + 1, rows, width), jnp.bfloat16),
            pltpu.VMEM((2, rows, width), jnp.float32),
            pltpu.VMEM((heads, span, size), jnp.bfloat16),
            pltpu.VMEM((heads, span, size), jnp.bfloat16),
            pltpu.SemaphoreType.DMA((1,)),
            pltpu.SemaphoreType.DMA((2, n // 2, 2)),
            pltpu.SemaphoreType.DMA((2, n // 2, 2)),
            pltpu.SemaphoreType.DMA((n, pairs)),
            pltpu.SemaphoreType.DMA((n, pairs)),
        ],
        compiler_params=pltpu.CompilerParams(
            collective_id=1, has_side_effects=True, vmem_limit_bytes=VMEM_BYTES
        ),
        name="attend_scatter",
    )(start, queries, kv, k_old, v_old, cosine, sine, w_out)


def local(n, snake, tokens, w_query, w_key, w_value, w_out, k_cache, v_cache, span_start):
    span = n * tokens.shape[0]
    positions = span_start[0] + jnp.arange(span, dtype=jnp.int32)
    cosine, sine = rope_tables(positions, k_cache.shape[2])
    queries, kv, k_old, v_old = gather_project(
        tokens, w_query, w_key.T, w_value.T, k_cache, v_cache, cosine, sine, n, snake
    )
    return attend_scatter(
        span_start, queries, kv, k_old, v_old, cosine, sine, w_out, n, snake
    )


def solution(mesh):
    n = mesh.shape["din"]
    snake = n == 8
    return jax.shard_map(
        functools.partial(local, n, snake),
        mesh=mesh,
        in_specs=(
            P(("groups", "din"), "dout"),
            P("dout", "din"),
            P("dout", "din"),
            P("dout", "din"),
            P("din", "dout"),
            P("groups", "din", None),
            P("groups", "din", None),
            P("groups"),
        ),
        out_specs=P(("groups", "din"), "dout"),
        check_vma=False,
    )
```
